32 devices in a mesh: section: 4 (over x, core), seq: 2 (over y), tp: 4 (over z).
Axes of the slice: x: 2, y: 2, z: 4, core: 2. Of those that a mesh axis runs over, the one named last changes fastest.
Arguments:
- frames: bfloat16 [4, 2048, 1536], P('section', ('seq', 'tp')), may hold values from -64 to 64
- pointwise_in: bfloat16 [1536, 3072], P(None, 'tp'), may hold values from -0.15625 to 0.15625
- depth_kernel: float32 [31, 1536], P(None, 'tp'), may hold values from -1 to 1
- norm_scale: float32 [1536], P('tp'), may hold values from 0.5 to 2
- norm_shift: float32 [1536], P('tp'), may hold values from -3 to 3
- pointwise_out: bfloat16 [1536, 1536], P('tp'), may hold values from -0.21875 to 0.21875
- adapter_weight: bfloat16 [6144, 8192], P(('section', 'seq'), 'tp'), may hold values from -0.078125 to 0.078125
Outputs:
- arrival: bfloat16 [4, 512, 8192], P('section', 'seq', 'tp')
The draws below stay inside these ranges and needn't reach their ends.
All inputs are finite; a program needn't handle non-finite values.
Results may differ from the reference program's by a relative error of at most 0.01.
Values may be sent and summed in bfloat16 or wider, within the bound.
A program may use at most 128 MiB of HBM per device.

```python
import math
import jax
import jax.numpy as jnp
from jax import lax

C = 1536
K = 31
D = 8192
STACK = 4
MB = 4
FRAMES = 2048
TOKENS = 512
N_TP = 4


def draw_frames(key, part):
    subkeys = jax.random.split(key, 3)
    channel_scale = jnp.exp(jax.random.uniform(subkeys[0], (1, 1, C), jnp.float32, math.log(0.4), math.log(4.0)))
    frame_scale = jnp.exp(jax.random.uniform(subkeys[1], (MB, FRAMES, 1), jnp.float32, math.log(0.4), math.log(4.0)))
    baseline = jnp.clip(jax.random.normal(subkeys[2], (MB, FRAMES, C), jnp.float32), -4.0, 4.0)
    return (baseline * channel_scale * frame_scale).astype(jnp.bfloat16)


def strengthened(drawn, key, source, target, parts, factor):
    def block_of(axis_at):
        return (jnp.arange(drawn.shape[axis_at]) // (drawn.shape[axis_at] // parts)).reshape((-1,) + (1,) * (drawn.ndim - 1 - axis_at))

    first = jax.random.permutation(key, parts)[block_of(target)]
    second = (block_of(target) + parts // 2) % parts
    return jnp.where((block_of(source) == first) | (block_of(source) == second), factor * drawn, drawn)


def block_scale(key, extent, pieces, least, high):
    def one(dim, blocks):
        heights = jax.random.uniform(jax.random.fold_in(jax.random.fold_in(key, 6), dim), (blocks,), jnp.float32, least / len(pieces), high / len(pieces))
        return jnp.repeat(jnp.exp(heights), extent[dim] // blocks).reshape((-1,) + (1,) * (len(extent) - dim - 1))

    gain = one(*pieces[0])
    for cut in pieces[1:]:
        gain = gain * one(*cut)
    return gain


def noise(key, extent, spread, bound, pieces=(), dtype=jnp.bfloat16):
    array = spread * jax.random.normal(key, extent, jnp.float32)
    if pieces:
        array = array * block_scale(key, extent, pieces, -0.22, 0.18)
    return jnp.clip(array, -bound, bound).astype(dtype)


def bell_draw_with(key, shape, scale, bound, pieces, heavy, held_as=jnp.bfloat16):
    array = scale * jax.random.normal(key, shape, jnp.float32)
    if pieces:
        array = array * block_scale(key, shape, pieces, -0.22, 0.18)
    return jnp.clip(strengthened(array, jax.random.fold_in(key, 3), *heavy), -bound, bound).astype(held_as)


def setup_inputs(seed: int = 0) -> dict:
    seeds = jax.random.split(jax.random.key(seed), 8)
    frames = draw_frames(jax.random.fold_in(seeds[7], 71), 0)
    pointwise_in = noise(seeds[1], (C, 2 * C), C ** -0.5, 0.15625, ((1, 4),))
    depth_kernel = noise(seeds[2], (K, C), K ** -0.5, 1.0, ((1, 4),), jnp.float32)
    norm_scale = jnp.clip(jnp.exp(math.log(2.0) - 1.3862944 * jax.random.uniform(seeds[3], (C,), jnp.float32) ** block_scale(seeds[3], (C,), ((0, 4),), -0.2, 0.2)), 0.5, 2.0)
    norm_shift = noise(seeds[4], (C,), 0.5, 3.0, ((0, 4),), jnp.float32)
    pointwise_out = bell_draw_with(seeds[5], (C, C), C ** -0.5, 0.21875, ((0, 4),), (0, 1, 4, 2.0))
    adapter_weight = noise(seeds[6], (STACK * C, D), (STACK * C) ** -0.5, 0.078125, ((0, 8), (1, 4)))
    return dict(frames=frames, pointwise_in=pointwise_in, depth_kernel=depth_kernel, norm_scale=norm_scale, norm_shift=norm_shift, pointwise_out=pointwise_out, adapter_weight=adapter_weight)


norm_eps = 1e-05

def encode_one(frames_one, pointwise_in, depth_kernel, norm_scale, norm_shift, pointwise_out, adapter_weight):
    signal = frames_one.astype(jnp.float32)
    centred = signal - lax.optimization_barrier(jnp.mean(signal, axis=-1, keepdims=True))
    variance = lax.optimization_barrier(jnp.mean(centred * centred, axis=-1, keepdims=True))
    normed = (centred * lax.rsqrt(variance + norm_eps)).astype(jnp.bfloat16)
    block_width = C // N_TP
    arranged = pointwise_in.reshape(C, N_TP, 2, block_width)
    value_w = arranged[:, :, 0, :].reshape(C, C)
    gate_w = arranged[:, :, 1, :].reshape(C, C)
    value_part = jnp.dot(normed, value_w, preferred_element_type=jnp.float32)
    gate_part = jnp.dot(normed, gate_w, preferred_element_type=jnp.float32)
    gated = (value_part * jax.nn.sigmoid(gate_part)).astype(jnp.bfloat16)
    half_width = (K - 1) // 2
    padded = jnp.pad(gated.astype(jnp.float32), ((half_width, half_width), (0, 0)))
    filtered = jnp.zeros((FRAMES, C), jnp.float32)
    for offset in range(K):
        filtered = filtered + padded[offset:offset + FRAMES] * depth_kernel[offset]
    activated = jax.nn.silu(filtered * norm_scale + norm_shift).astype(jnp.bfloat16)
    mixed = jnp.zeros((FRAMES, C), jnp.float32)
    for member in range(N_TP):
        lower = member * block_width
        partial_value = jnp.dot(activated[:, lower:lower + block_width], pointwise_out[lower:lower + block_width], preferred_element_type=jnp.float32)
        rounded = lax.optimization_barrier(partial_value.astype(jnp.bfloat16))
        mixed = mixed + rounded.astype(jnp.float32)
    encoded = (signal + mixed).astype(jnp.bfloat16)
    stacked = encoded.reshape(TOKENS, STACK * C)
    return jnp.dot(stacked, adapter_weight, preferred_element_type=jnp.float32).astype(jnp.bfloat16)

def reference(frames, pointwise_in, depth_kernel, norm_scale, norm_shift, pointwise_out, adapter_weight):

    def one_batch(frames_one):
        return encode_one(frames_one, pointwise_in, depth_kernel, norm_scale, norm_shift, pointwise_out, adapter_weight)
    bridged = lax.map(one_batch, frames)
    return jnp.roll(bridged, 1, axis=0)
```

```python
import jax
import jax.numpy as jnp
from jax import lax
from jax.sharding import PartitionSpec as P

STACK = 4
HALO = 16

norm_eps = 1e-05


def layer_norm_rows(signal):
    centred = signal - jnp.mean(signal, axis=-1, keepdims=True)
    variance = jnp.mean(centred * centred, axis=-1, keepdims=True)
    return (centred * lax.rsqrt(variance + norm_eps)).astype(jnp.bfloat16)


def own_piece(array, count, index):
    rows = array.shape[0] // count
    return lax.dynamic_slice_in_dim(array, index * rows, rows, 0)


def per_device(
    frames, pointwise_in, depth_kernel, norm_scale, norm_shift, pointwise_out, adapter_weight
):
    tp = lax.axis_size("tp")
    copies = lax.axis_size("section") * lax.axis_size("seq")
    copy_index = lax.axis_index("section") * lax.axis_size("seq") + lax.axis_index("seq")
    everywhere = ("tp", "section", "seq")
    rows = frames.shape[1]
    channels = frames.shape[2]
    block = channels // tp
    taps = depth_kernel.shape[0]
    half_width = (taps - 1) // 2

    own = frames[0]
    count = lax.axis_size("seq") * tp
    before = lax.ppermute(own[rows - HALO :], ("seq", "tp"), [(i, i + 1) for i in range(count - 1)])
    after = lax.ppermute(own[:HALO], ("seq", "tp"), [(i + 1, i) for i in range(count - 1)])

    small = jnp.concatenate([depth_kernel, norm_scale[None], norm_shift[None]], axis=0)
    small = lax.all_gather(small, "tp", axis=0)
    small = jnp.swapaxes(small, 0, 1).reshape(taps + 2, channels)
    win = lax.all_gather(own_piece(pointwise_in, copies, copy_index), everywhere, axis=0, tiled=True)
    win = win.reshape(tp, channels, 2 * block)
    wout = lax.all_gather(own_piece(pointwise_out, copies, copy_index), everywhere, axis=0, tiled=True)

    extended = jnp.concatenate([before, own, after], axis=0).astype(jnp.float32)
    normed = layer_norm_rows(extended)
    gated = []
    for b in range(tp):
        projected = jnp.dot(normed, win[b], preferred_element_type=jnp.float32)
        gated.append(
            (projected[:, :block] * jax.nn.sigmoid(projected[:, block:])).astype(jnp.bfloat16)
        )
    padded = jnp.concatenate(gated, axis=1)
    filtered = jnp.zeros((rows, channels), jnp.float32)
    first = HALO - half_width
    for offset in range(taps):
        filtered = filtered + padded[first + offset : first + offset + rows] * small[offset]
    activated = jax.nn.silu(filtered * small[taps] + small[taps + 1]).astype(jnp.bfloat16)
    mixed = jnp.dot(activated, wout, preferred_element_type=jnp.float32)
    encoded = (own.astype(jnp.float32) + mixed).astype(jnp.bfloat16)
    stacked = encoded.reshape(rows // STACK, STACK * channels)
    stacked = lax.all_gather(stacked, "tp", axis=0, tiled=True)
    weight = lax.all_gather(adapter_weight, ("section", "seq"), axis=0, tiled=True)
    bridged = jnp.dot(stacked, weight, preferred_element_type=jnp.float32).astype(jnp.bfloat16)
    sections = lax.axis_size("section")
    return lax.ppermute(
        bridged[None], "section", [(i, (i + 1) % sections) for i in range(sections)]
    )


def solution(mesh):
    placed = (
        P("section", ("seq", "tp"), None),
        P(None, "tp"),
        P(None, "tp"),
        P("tp"),
        P("tp"),
        P("tp", None),
        P(("section", "seq"), "tp"),
    )
    return jax.shard_map(
        per_device, mesh=mesh, in_specs=placed, out_specs=P("section", "seq", "tp"), check_vma=False
    )
```

```python
import functools

import jax
import jax.numpy as jnp
from jax import lax
from jax.experimental import pallas as pl
from jax.experimental.pallas import tpu as pltpu
from jax.sharding import PartitionSpec as P

STACK = 4
HALO = 16
MESH = pl.DeviceIdType.MESH

norm_eps = 1e-05


def layer_norm_rows(signal):
    centred = signal - jnp.mean(signal, axis=-1, keepdims=True)
    variance = jnp.mean(centred * centred, axis=-1, keepdims=True)
    return (centred * lax.rsqrt(variance + norm_eps)).astype(jnp.bfloat16)


def own_piece(array, count, index):
    rows = array.shape[0] // count
    return lax.dynamic_slice_in_dim(array, index * rows, rows, 0)


def adapter_kernel(
    axes, tile, enc_ref, w_ref, out_ref,
    wbuf, tok, psend, precv,
    w_sem, w_send, w_recv, a_send, right_send, left_send, tok_recv, p_send, p_recv,
):
    sections, seqs, depth = axes
    section, seq, layer = lax.axis_index("section"), lax.axis_index("seq"), lax.axis_index("tp")
    core, side = section % 2, section // 2
    sides = sections // 2
    after = (section + 1) % sections
    steps = [(i, j) for i in range(sides) for j in range(seqs)]
    steps = steps[1:][::-1] + steps[:1]
    groups = len(steps)
    tiles = out_ref.shape[1] // tile

    barrier = pltpu.get_barrier_semaphore()
    for i in range(sections):
        for j in range(seqs):
            if i + j > 0:
                pl.semaphore_signal(
                    barrier, inc=1, device_id_type=MESH,
                    device_id=((section + i) % sections, (seq + j) % seqs, layer),
                )

    @pl.when(layer > 0)
    def _():
        pl.semaphore_signal(
            barrier, inc=1, device_id=(section, seq, layer - 1), device_id_type=MESH
        )

    @pl.when(layer < depth - 1)
    def _():
        pl.semaphore_signal(
            barrier, inc=1, device_id=(section, seq, layer + 1), device_id_type=MESH
        )

    neighbours = (layer + depth - 1) // depth + (2 * depth - 2 - layer) // depth
    pl.semaphore_wait(barrier, sections * seqs - 1 + neighbours)

    def remote(src, dst, send, recv, target):
        return pltpu.make_async_remote_copy(
            src_ref=src, dst_ref=dst, send_sem=send, recv_sem=recv,
            device_id=target, device_id_type=MESH,
        )

    own_w = pltpu.make_async_copy(w_ref, wbuf.at[core], w_sem)
    own_w.start()

    def a_copy(g):
        i, j = steps[g]
        to_side = (after // 2 - i + sides) % sides
        to_seq = (seq - j + seqs) % seqs
        return remote(
            enc_ref.at[pl.ds(2 * to_side, 2), to_seq], tok.at[g, layer],
            a_send.at[g], tok_recv.at[g, layer], (2 * to_side + after % 2, to_seq, layer),
        )

    for g in range(groups):
        a_copy(g).start()
    other_w = remote(
        w_ref, wbuf.at[core], w_send, w_recv, (section + 1 - 2 * core, seq, layer)
    )
    other_w.start()

    def pass_right(g, origin):
        return remote(
            tok.at[g, origin], tok.at[g, origin], right_send.at[g, origin],
            tok_recv.at[g, origin], (section, seq, layer + 1),
        )

    def pass_left(g, origin):
        return remote(
            tok.at[g, origin], tok.at[g, origin], left_send.at[g, origin],
            tok_recv.at[g, origin], (section, seq, layer - 1),
        )

    def arrived(g, origin):
        remote(
            tok.at[g, origin], tok.at[g, origin], a_send.at[g],
            tok_recv.at[g, origin], (section + 1 - 2 * core, seq, layer),
        ).wait_recv()

    def pass_both(g):
        arrived(g, layer)

        @pl.when(layer < depth - 1)
        def _():
            pass_right(g, layer).start()

        @pl.when(layer > 0)
        def _():
            pass_left(g, layer).start()

    def p_copy(g, t):
        i, j = steps[g]
        columns = pl.ds(pl.multiple_of(t * tile, tile), tile)
        to_side = (side + i) % sides
        return remote(
            psend.at[g, :, columns], precv.at[g, :, columns],
            p_send.at[g, t], p_recv.at[g, t], (2 * to_side + core, (seq + j) % seqs, layer),
        )

    def product(g, columns):
        shape = (depth * tok.shape[3], tok.shape[4])
        total = jnp.dot(
            tok[g, :, 0].reshape(shape), wbuf[0, :, columns], preferred_element_type=jnp.float32
        )
        return total + jnp.dot(
            tok[g, :, 1].reshape(shape), wbuf[1, :, columns], preferred_element_type=jnp.float32
        )

    pass_both(0)
    pass_both(1)
    for g in range(groups):
        for hop in range(1, depth):

            @pl.when(layer - hop >= 0)
            def _():
                arrived(g, layer - hop)

                @pl.when(layer < depth - 1)
                def _():
                    pass_right(g, layer - hop).start()

            @pl.when(layer + hop < depth)
            def _():
                arrived(g, layer + hop)

                @pl.when(layer > 0)
                def _():
                    pass_left(g, layer + hop).start()

        if g + 2 < groups:
            pass_both(g + 2)
        if g == 0:
            own_w.wait()
            other_w.wait()

        if g < groups - 1:

            @pl.loop(0, tiles)
            def _(t):
                columns = pl.ds(pl.multiple_of(t * tile, tile), tile)
                psend[g, :, columns] = product(g, columns).astype(jnp.bfloat16)
                p_copy(g, t).start()

        else:

            @pl.loop(0, tiles)
            def _(t):
                columns = pl.ds(pl.multiple_of(t * tile, tile), tile)
                total = product(g, columns)
                for k in range(groups - 1):
                    p_copy(k, t).wait_recv()
                    total = total + precv[k, :, columns].astype(jnp.float32)
                out_ref[:, columns] = total.astype(jnp.bfloat16)

    for g in range(groups):
        a_copy(g).wait_send()
        for origin in range(depth):

            @pl.when((layer < depth - 1) & (origin <= layer))
            def _():
                pass_right(g, origin).wait_send()

            @pl.when((layer > 0) & (origin >= layer))
            def _():
                pass_left(g, origin).wait_send()

        if g < groups - 1:

            @pl.loop(0, tiles)
            def _(t):
                p_copy(g, t).wait_send()


def adapter(enc, weight, tokens):
    axes = (lax.axis_size("section"), lax.axis_size("seq"), lax.axis_size("tp"))
    sections, seqs, depth = axes
    groups = sections // 2 * seqs
    few, width = enc.shape[2:]
    columns = weight.shape[1]
    tile = 512
    tiles = columns // tile
    dma = pltpu.SemaphoreType.DMA
    return pl.pallas_call(
        functools.partial(adapter_kernel, axes, tile),
        out_shape=jax.ShapeDtypeStruct((tokens, columns), jnp.bfloat16),
        in_specs=[pl.BlockSpec(memory_space=pltpu.VMEM), pl.BlockSpec(memory_space=pl.ANY)],
        out_specs=pl.BlockSpec(memory_space=pltpu.VMEM),
        scratch_shapes=[
            pltpu.VMEM((2, width, columns), jnp.bfloat16),
            pltpu.VMEM((groups, depth, 2, few, width), jnp.bfloat16),
            pltpu.VMEM((groups - 1, tokens, columns), jnp.bfloat16),
            pltpu.VMEM((groups - 1, tokens, columns), jnp.bfloat16),
            dma, dma, dma, dma((groups,)), dma((groups, depth)), dma((groups, depth)),
            dma((groups, depth)), dma((groups - 1, tiles)), dma((groups - 1, tiles)),
        ],
        compiler_params=pltpu.CompilerParams(
            collective_id=0, has_side_effects=True, vmem_limit_bytes=48 * 2**20
        ),
    )(enc, weight)


def per_device(
    frames, pointwise_in, depth_kernel, norm_scale, norm_shift, pointwise_out, adapter_weight
):
    tp = lax.axis_size("tp")
    copies = lax.axis_size("section") * lax.axis_size("seq")
    copy_index = lax.axis_index("section") * lax.axis_size("seq") + lax.axis_index("seq")
    everywhere = ("tp", "section", "seq")
    rows = frames.shape[1]
    channels = frames.shape[2]
    block = channels // tp
    taps = depth_kernel.shape[0]
    half_width = (taps - 1) // 2

    own = frames[0]
    count = lax.axis_size("seq") * tp
    before = lax.ppermute(own[rows - HALO :], ("seq", "tp"), [(i, i + 1) for i in range(count - 1)])
    after = lax.ppermute(own[:HALO], ("seq", "tp"), [(i + 1, i) for i in range(count - 1)])

    small = jnp.concatenate([depth_kernel, norm_scale[None], norm_shift[None]], axis=0)
    small = lax.all_gather(small, "tp", axis=0)
    small = jnp.swapaxes(small, 0, 1).reshape(taps + 2, channels)
    win = lax.all_gather(own_piece(pointwise_in, copies, copy_index), everywhere, axis=0, tiled=True)
    win = win.reshape(tp, channels, 2 * block)
    wout = lax.all_gather(own_piece(pointwise_out, copies, copy_index), everywhere, axis=0, tiled=True)

    extended = jnp.concatenate([before, own, after], axis=0).astype(jnp.float32)
    normed = layer_norm_rows(extended)
    gated = []
    for b in range(tp):
        projected = jnp.dot(normed, win[b], preferred_element_type=jnp.float32)
        gated.append(
            (projected[:, :block] * jax.nn.sigmoid(projected[:, block:])).astype(jnp.bfloat16)
        )
    padded = jnp.concatenate(gated, axis=1)
    filtered = jnp.zeros((rows, channels), jnp.float32)
    first = HALO - half_width
    for offset in range(taps):
        filtered = filtered + padded[first + offset : first + offset + rows] * small[offset]
    activated = jax.nn.silu(filtered * small[taps] + small[taps + 1]).astype(jnp.bfloat16)
    mixed = jnp.dot(activated, wout, preferred_element_type=jnp.float32)
    encoded = (own.astype(jnp.float32) + mixed).astype(jnp.bfloat16)
    seqs = lax.axis_size("seq")
    enc = encoded.reshape(rows // STACK, STACK, seqs, channels // seqs)
    enc = jnp.transpose(enc, (1, 2, 0, 3))
    return adapter(enc, adapter_weight, rows // STACK * tp)[None]


def solution(mesh):
    placed = (
        P("section", ("seq", "tp"), None),
        P(None, "tp"),
        P(None, "tp"),
        P("tp"),
        P("tp"),
        P("tp", None),
        P(("section", "seq"), "tp"),
    )
    return jax.shard_map(
        per_device, mesh=mesh, in_specs=placed, out_specs=P("section", "seq", "tp"), check_vma=False
    )
```

```python
import functools

import jax
import jax.numpy as jnp
from jax import lax
from jax.experimental import pallas as pl
from jax.experimental.pallas import tpu as pltpu
from jax.sharding import PartitionSpec as P

STACK = 4
HALO = 16
MESH = pl.DeviceIdType.MESH

norm_eps = 1e-05


def layer_norm_rows(signal):
    centred = signal - jnp.mean(signal, axis=-1, keepdims=True)
    variance = jnp.mean(centred * centred, axis=-1, keepdims=True)
    return (centred * lax.rsqrt(variance + norm_eps)).astype(jnp.bfloat16)


def own_piece(array, count, index):
    rows = array.shape[0] // count
    return lax.dynamic_slice_in_dim(array, index * rows, rows, 0)


def adapter_kernel(
    axes, tile, enc_ref, w_ref, out_ref,
    wbuf, tok, psend, precv,
    w_sem, w_send, w_recv, a_send, right_send, left_send, tok_recv, p_send, p_recv,
):
    sections, seqs, depth = axes
    section, seq, layer = lax.axis_index("section"), lax.axis_index("seq"), lax.axis_index("tp")
    core, side = section % 2, section // 2
    sides = sections // 2
    after = (section + 1) % sections
    steps = [(i, j) for i in range(sides) for j in range(seqs)]
    steps = steps[1:][::-1] + steps[:1]
    groups = len(steps)
    tiles = out_ref.shape[1] // tile

    barrier = pltpu.get_barrier_semaphore()
    for i in range(sections):
        for j in range(seqs):
            if i + j > 0:
                pl.semaphore_signal(
                    barrier, inc=1, device_id_type=MESH,
                    device_id=((section + i) % sections, (seq + j) % seqs, layer),
                )

    @pl.when(layer > 0)
    def _():
        pl.semaphore_signal(
            barrier, inc=1, device_id=(section, seq, layer - 1), device_id_type=MESH
        )

    @pl.when(layer < depth - 1)
    def _():
        pl.semaphore_signal(
            barrier, inc=1, device_id=(section, seq, layer + 1), device_id_type=MESH
        )

    neighbours = (layer + depth - 1) // depth + (2 * depth - 2 - layer) // depth
    pl.semaphore_wait(barrier, sections * seqs - 1 + neighbours)

    def remote(src, dst, send, recv, target):
        return pltpu.make_async_remote_copy(
            src_ref=src, dst_ref=dst, send_sem=send, recv_sem=recv,
            device_id=target, device_id_type=MESH,
        )

    own_w = pltpu.make_async_copy(w_ref, wbuf.at[core], w_sem)
    own_w.start()

    def a_copy(g):
        i, j = steps[g]
        to_side = (after // 2 - i + sides) % sides
        to_seq = (seq - j + seqs) % seqs
        return remote(
            enc_ref.at[pl.ds(2 * to_side, 2), to_seq], tok.at[g, layer],
            a_send.at[g], tok_recv.at[g, layer], (2 * to_side + after % 2, to_seq, layer),
        )

    for g in range(groups):
        a_copy(g).start()
    other_w = remote(
        w_ref, wbuf.at[core], w_send, w_recv, (section + 1 - 2 * core, seq, layer)
    )
    other_w.start()

    def pass_right(g, origin):
        return remote(
            tok.at[g, origin], tok.at[g, origin], right_send.at[g, origin],
            tok_recv.at[g, origin], (section, seq, layer + 1),
        )

    def pass_left(g, origin):
        return remote(
            tok.at[g, origin], tok.at[g, origin], left_send.at[g, origin],
            tok_recv.at[g, origin], (section, seq, layer - 1),
        )

    def arrived(g, origin):
        remote(
            tok.at[g, origin], tok.at[g, origin], a_send.at[g],
            tok_recv.at[g, origin], (section + 1 - 2 * core, seq, layer),
        ).wait_recv()

    def pass_both(g):
        arrived(g, layer)

        @pl.when(layer < depth - 1)
        def _():
            pass_right(g, layer).start()

        @pl.when(layer > 0)
        def _():
            pass_left(g, layer).start()

    def p_copy(g, t):
        i, j = steps[g]
        columns = pl.ds(pl.multiple_of(t * tile, tile), tile)
        to_side = (side + i) % sides
        return remote(
            psend.at[g, :, columns], precv.at[g, :, columns],
            p_send.at[g, t], p_recv.at[g, t], (2 * to_side + core, (seq + j) % seqs, layer),
        )

    def product(g, columns):
        shape = (depth * tok.shape[3], tok.shape[4])
        total = jnp.dot(
            tok[g, :, 0].reshape(shape), wbuf[0, :, columns], preferred_element_type=jnp.float32
        )
        return total + jnp.dot(
            tok[g, :, 1].reshape(shape), wbuf[1, :, columns], preferred_element_type=jnp.float32
        )

    pass_both(0)
    pass_both(1)
    for g in range(groups):
        for hop in range(1, depth):

            @pl.when(layer - hop >= 0)
            def _():
                arrived(g, layer - hop)

                @pl.when(layer < depth - 1)
                def _():
                    pass_right(g, layer - hop).start()

            @pl.when(layer + hop < depth)
            def _():
                arrived(g, layer + hop)

                @pl.when(layer > 0)
                def _():
                    pass_left(g, layer + hop).start()

        if g + 2 < groups:
            pass_both(g + 2)
        if g == 0:
            own_w.wait()
            other_w.wait()

        if g < groups - 1:

            @pl.loop(0, tiles)
            def _(t):
                columns = pl.ds(pl.multiple_of(t * tile, tile), tile)
                psend[g, :, columns] = product(g, columns).astype(jnp.bfloat16)
                p_copy(g, t).start()

        else:

            @pl.loop(0, tiles)
            def _(t):
                columns = pl.ds(pl.multiple_of(t * tile, tile), tile)
                total = product(g, columns)
                for k in range(groups - 1):
                    p_copy(k, t).wait_recv()
                    total = total + precv[k, :, columns].astype(jnp.float32)
                out_ref[:, columns] = total.astype(jnp.bfloat16)

    for g in range(groups):
        a_copy(g).wait_send()
        for origin in range(depth):

            @pl.when((layer < depth - 1) & (origin <= layer))
            def _():
                pass_right(g, origin).wait_send()

            @pl.when((layer > 0) & (origin >= layer))
            def _():
                pass_left(g, origin).wait_send()

        if g < groups - 1:

            @pl.loop(0, tiles)
            def _(t):
                p_copy(g, t).wait_send()


def adapter(enc, weight, tokens):
    axes = (lax.axis_size("section"), lax.axis_size("seq"), lax.axis_size("tp"))
    sections, seqs, depth = axes
    groups = sections // 2 * seqs
    few, width = enc.shape[2:]
    columns = weight.shape[1]
    tile = 512
    tiles = columns // tile
    dma = pltpu.SemaphoreType.DMA
    return pl.pallas_call(
        functools.partial(adapter_kernel, axes, tile),
        out_shape=jax.ShapeDtypeStruct((tokens, columns), jnp.bfloat16),
        in_specs=[pl.BlockSpec(memory_space=pltpu.VMEM), pl.BlockSpec(memory_space=pl.ANY)],
        out_specs=pl.BlockSpec(memory_space=pltpu.VMEM),
        scratch_shapes=[
            pltpu.VMEM((2, width, columns), jnp.bfloat16),
            pltpu.VMEM((groups, depth, 2, few, width), jnp.bfloat16),
            pltpu.VMEM((groups - 1, tokens, columns), jnp.bfloat16),
            pltpu.VMEM((groups - 1, tokens, columns), jnp.bfloat16),
            dma, dma, dma, dma((groups,)), dma((groups, depth)), dma((groups, depth)),
            dma((groups, depth)), dma((groups - 1, tiles)), dma((groups - 1, tiles)),
        ],
        compiler_params=pltpu.CompilerParams(
            collective_id=0, has_side_effects=True, vmem_limit_bytes=48 * 2**20
        ),
    )(enc, weight)


def gather_kernel(
    axes, piece_ref, out_ref, own_sem, right_send, left_send, plane_send, core_send, recv
):
    sections, seqs, depth = axes
    section, seq, layer = lax.axis_index("section"), lax.axis_index("seq"), lax.axis_index("tp")
    core = section % 2
    me = section * seqs + seq
    steps = [(2 * i, j) for i in range(sections // 2) for j in range(seqs)][:0:-1]

    barrier = pltpu.get_barrier_semaphore()
    for i in range(sections):
        for j in range(seqs):
            if i + j > 0:
                pl.semaphore_signal(
                    barrier, inc=1, device_id_type=MESH,
                    device_id=((section + i) % sections, (seq + j) % seqs, layer),
                )

    @pl.when(layer > 0)
    def _():
        pl.semaphore_signal(
            barrier, inc=1, device_id=(section, seq, layer - 1), device_id_type=MESH
        )

    @pl.when(layer < depth - 1)
    def _():
        pl.semaphore_signal(
            barrier, inc=1, device_id=(section, seq, layer + 1), device_id_type=MESH
        )

    neighbours = (layer + depth - 1) // depth + (2 * depth - 2 - layer) // depth
    pl.semaphore_wait(barrier, sections * seqs - 1 + neighbours)

    def send(origin, rank, sem, target):
        return pltpu.make_async_remote_copy(
            src_ref=out_ref.at[origin, rank], dst_ref=out_ref.at[origin, rank],
            send_sem=sem, recv_sem=recv.at[origin, rank],
            device_id=target, device_id_type=MESH,
        )

    def right(origin):
        return send(origin, me, right_send.at[origin], (section, seq, layer + 1))

    def left(origin):
        return send(origin, me, left_send.at[origin], (section, seq, layer - 1))

    def plane(origin, k):
        i, j = steps[k]
        target = ((section + i) % sections, (seq + j) % seqs, layer)
        return send(origin, me, plane_send.at[origin, k], target)

    def across(origin, rank):
        return send(
            origin, rank, core_send.at[origin, rank], (section + 1 - 2 * core, seq, layer)
        )

    def spread(origin):
        for k in range(len(steps)):
            plane(origin, k).start()
        across(origin, me).start()

    def peer(k):
        i, j = steps[k]
        return (section + i) % sections * seqs + (seq + j) % seqs

    own = pltpu.make_async_copy(piece_ref, out_ref.at[layer, me], own_sem)
    own.start()
    own.wait()

    @pl.when(layer < depth - 1)
    def _():
        right(layer).start()

    @pl.when(layer > 0)
    def _():
        left(layer).start()

    spread(layer)

    def relay(origin):
        for k in range(len(steps)):
            across(origin, peer(k)).wait_recv()
            across(origin, peer(k)).start()

    for hop in range(1, depth):

        @pl.when(layer - hop >= 0)
        def _():
            across(layer - hop, me).wait_recv()

            @pl.when(layer < depth - 1)
            def _():
                right(layer - hop).start()

            spread(layer - hop)

        @pl.when(layer + hop < depth)
        def _():
            across(layer + hop, me).wait_recv()

            @pl.when(layer > 0)
            def _():
                left(layer + hop).start()

            spread(layer + hop)

        if hop == 1:
            relay(layer)
        else:

            @pl.when(layer - hop + 1 >= 0)
            def _():
                relay(layer - hop + 1)

            @pl.when(layer + hop - 1 < depth)
            def _():
                relay(layer + hop - 1)

    @pl.when(layer - depth + 1 >= 0)
    def _():
        relay(layer - depth + 1)

    @pl.when(layer + depth - 1 < depth)
    def _():
        relay(layer + depth - 1)

    for origin in range(depth):

        @pl.when((layer < depth - 1) & (origin <= layer))
        def _():
            right(origin).wait_send()

        @pl.when((layer > 0) & (origin >= layer))
        def _():
            left(origin).wait_send()

        for k in range(len(steps)):
            plane(origin, k).wait_send()
        for i in range(0, sections, 2):
            for j in range(seqs):
                across(origin, (i + core) * seqs + j).wait_send()
                across(origin, (i + 1 - core) * seqs + j).wait_recv()


def gathered_everywhere(piece):
    axes = (lax.axis_size("section"), lax.axis_size("seq"), lax.axis_size("tp"))
    sections, seqs, depth = axes
    copies = sections * seqs
    dma = pltpu.SemaphoreType.DMA
    return pl.pallas_call(
        functools.partial(gather_kernel, axes),
        out_shape=jax.ShapeDtypeStruct((depth, copies) + piece.shape, piece.dtype),
        in_specs=[pl.BlockSpec(memory_space=pl.ANY)],
        out_specs=pl.BlockSpec(memory_space=pl.ANY),
        scratch_shapes=[
            dma, dma((depth,)), dma((depth,)), dma((depth, copies // 2 - 1)),
            dma((depth, copies)), dma((depth, copies)),
        ],
        compiler_params=pltpu.CompilerParams(collective_id=1, has_side_effects=True),
    )(piece)


def per_device(
    frames, pointwise_in, depth_kernel, norm_scale, norm_shift, pointwise_out, adapter_weight
):
    tp = lax.axis_size("tp")
    copies = lax.axis_size("section") * lax.axis_size("seq")
    copy_index = lax.axis_index("section") * lax.axis_size("seq") + lax.axis_index("seq")
    everywhere = ("tp", "section", "seq")
    rows = frames.shape[1]
    channels = frames.shape[2]
    block = channels // tp
    taps = depth_kernel.shape[0]
    half_width = (taps - 1) // 2

    own = frames[0]
    count = lax.axis_size("seq") * tp
    before = lax.ppermute(own[rows - HALO :], ("seq", "tp"), [(i, i + 1) for i in range(count - 1)])
    after = lax.ppermute(own[:HALO], ("seq", "tp"), [(i + 1, i) for i in range(count - 1)])

    small = jnp.concatenate([depth_kernel, norm_scale[None], norm_shift[None]], axis=0)
    small = lax.all_gather(small, "tp", axis=0)
    small = jnp.swapaxes(small, 0, 1).reshape(taps + 2, channels)
    first_piece = own_piece(pointwise_in, copies, copy_index)
    second_piece = own_piece(pointwise_out.reshape(-1, 2 * block), copies, copy_index)
    cut = first_piece.shape[0]
    weights = gathered_everywhere(jnp.concatenate([first_piece, second_piece], axis=0))
    win = weights[:, :, :cut].reshape(tp, channels, 2 * block)
    wout = weights[:, :, cut:].reshape(channels, channels)

    extended = jnp.concatenate([before, own, after], axis=0).astype(jnp.float32)
    normed = layer_norm_rows(extended)
    gated = []
    for b in range(tp):
        projected = jnp.dot(normed, win[b], preferred_element_type=jnp.float32)
        gated.append(
            (projected[:, :block] * jax.nn.sigmoid(projected[:, block:])).astype(jnp.bfloat16)
        )
    padded = jnp.concatenate(gated, axis=1)
    filtered = jnp.zeros((rows, channels), jnp.float32)
    first = HALO - half_width
    for offset in range(taps):
        filtered = filtered + padded[first + offset : first + offset + rows] * small[offset]
    activated = jax.nn.silu(filtered * small[taps] + small[taps + 1]).astype(jnp.bfloat16)
    mixed = jnp.dot(activated, wout, preferred_element_type=jnp.float32)
    encoded = (own.astype(jnp.float32) + mixed).astype(jnp.bfloat16)
    seqs = lax.axis_size("seq")
    enc = encoded.reshape(rows // STACK, STACK, seqs, channels // seqs)
    enc = jnp.transpose(enc, (1, 2, 0, 3))
    return adapter(enc, adapter_weight, rows // STACK * tp)[None]


def solution(mesh):
    placed = (
        P("section", ("seq", "tp"), None),
        P(None, "tp"),
        P(None, "tp"),
        P("tp"),
        P("tp"),
        P("tp", None),
        P(("section", "seq"), "tp"),
    )
    return jax.shard_map(
        per_device, mesh=mesh, in_specs=placed, out_specs=P("section", "seq", "tp"), check_vma=False
    )
```
